32 devices in a mesh: member: 4 (over y, x), space: 8 (over z, core).
Axes of the slice: x: 2, y: 2, z: 4, core: 2. Of those that a mesh axis runs over, the one named last changes fastest.
Arguments:
- prior_samples: float32 [256, 64, 2048], P('member', 'space'), may hold values from -6 to 6
- external_drive: float32 [64, 2048], P('space'), may hold values from -6 to 6
- obs_value: float32 [8, 16, 1024], P('space', 'member'), may hold values from -6 to 6
- obs_index: int32 [8, 16, 1024], P('space', 'member'), may hold values from 0 to 1023
- obs_weight: bfloat16 [8, 16, 1024], P('space', 'member'), may hold values from 0.5 to 8
Outputs:
- analysis: float32 [256, 64, 2048], P('member', 'space')
The draws below stay inside these ranges and needn't reach their ends.
Inputs may be any that keep to these rules, and one draw needn't show every extreme that they name: `obs_index`: the cell is numbered row by row within the region: row times 128 plus column.
All inputs are finite; a program needn't handle non-finite values.
Results may differ from the reference program's by a relative error of at most 0.0017.
Values may be sent and summed in bfloat16 or wider, within the bound.
A program may use at most 128 MiB of HBM per device.

```python
import math
import jax
import jax.numpy as jnp
from jax import lax

SAMPLE_TOTAL = 256
STRIP_HEIGHT = 8
TILE_WIDTH = 128
OBS = 1024
STEPS = 8
ITERS = 6
ROWS = 64
COLS = 2048
COL_REGIONS = 16
N_SPACE = 8


def place_ends(result, rng, low, high):
    dims = result.shape
    spot = [jax.random.randint(jax.random.fold_in(rng, axis), (), 0, dims[axis]) for axis in range(len(dims))]
    result = result.at[tuple(spot)].set(low)
    longest = dims.index(max(dims))
    spot[longest] = (spot[longest] + 1) % dims[longest]
    return result.at[tuple(spot)].set(high)


def levels(stream_key, shape, pieces, smallest, largest):
    level, own = 1.0, jax.random.fold_in(stream_key, 6)
    for position, shards_of in pieces:
        draws = jnp.exp(jax.random.uniform(jax.random.fold_in(own, position), (shards_of,), jnp.float32, smallest / len(pieces), largest / len(pieces)))
        level = level * jnp.repeat(draws, shape[position] // shards_of).reshape([-1 if axis == position else 1 for axis in range(len(shape))])
    return level


def gaussian(own_key, shape, scale, limit, pieces=(), kind=jnp.bfloat16):
    level = levels(own_key, shape, pieces, -0.22, 0.18) if pieces else 1.0
    values = jax.random.normal(own_key, shape, jnp.float32) * scale * level
    return jnp.minimum(jnp.maximum(values, -limit), limit).astype(kind)


def setup_inputs(seed: int = 0) -> dict:
    splits = jax.random.split(jax.random.key(seed), 6)
    prior_samples = gaussian(splits[0], (SAMPLE_TOTAL, ROWS, COLS), 1.0, 6.0, ((0, 4), (1, 8)), jnp.float32)
    external_drive = gaussian(splits[1], (ROWS, COLS), 1.0, 6.0, ((0, 8),), jnp.float32)
    obs_value = gaussian(splits[2], (N_SPACE, COL_REGIONS, OBS), 1.0, 6.0, ((0, 8), (1, 4)), jnp.float32)
    obs_index = place_ends(jax.random.randint(splits[3], (N_SPACE, COL_REGIONS, OBS), 0, STRIP_HEIGHT * TILE_WIDTH), jax.random.fold_in(splits[3], 1), 0, (STRIP_HEIGHT * TILE_WIDTH) - 1).astype(jnp.int32)
    obs_weight = jnp.clip(jnp.exp(math.log(8.0) - 2.7725887 * jax.random.uniform(splits[4], (N_SPACE, COL_REGIONS, OBS), jnp.float32) ** levels(splits[4], (N_SPACE, COL_REGIONS, OBS), ((0, 8), (1, 4)), -0.2, 0.2)), 0.5, 8.0).astype(jnp.bfloat16)
    return {"prior_samples": prior_samples, "external_drive": external_drive, "obs_value": obs_value, "obs_index": obs_index, "obs_weight": obs_weight}


step_size = 0.1
vertical_diffusion = 4.0
lateral_diffusion = 0.5
damping = 0.5

def sample_prediction(sample_grid_vector, external_drive):
    for step_index in range(STEPS):
        padded = jnp.pad(sample_grid_vector, ((1, 1), (0, 0)))
        upper_rows = padded[:-2]
        lower_rows = padded[2:]
        right_cells = jnp.roll(sample_grid_vector, -1, axis=1)
        left_cells = jnp.roll(sample_grid_vector, 1, axis=1)
        laplace = vertical_diffusion * (upper_rows + lower_rows - 2.0 * sample_grid_vector) + lateral_diffusion * (right_cells + left_cells - 2.0 * sample_grid_vector)
        advect = sample_grid_vector * (right_cells - left_cells + (lower_rows - upper_rows)) * 0.5
        sample_grid_vector = sample_grid_vector + step_size * (laplace - advect - damping * sample_grid_vector + external_drive)
    return sample_grid_vector

def taper_above(row_pos, row_span):
    distance = row_span - row_pos
    return jnp.exp(-2.0 * distance * distance / (row_span * row_span))

def taper_below(row_pos, row_span):
    distance = row_pos + 1.0
    return jnp.exp(-2.0 * distance * distance / (row_span * row_span))

def reference(prior_samples, external_drive, obs_value, obs_index, obs_weight):
    highest = lax.Precision.HIGHEST
    predicted_field = lax.map(lambda sample_grid_vector: sample_prediction(sample_grid_vector, external_drive), prior_samples)
    lateral_tiles = COLS // TILE_WIDTH
    points_within_tile = STRIP_HEIGHT * TILE_WIDTH
    number_tiles = N_SPACE * lateral_tiles
    vertical_strips = predicted_field.reshape(SAMPLE_TOTAL, N_SPACE, STRIP_HEIGHT, lateral_tiles, TILE_WIDTH).transpose(1, 3, 0, 2, 4).reshape(number_tiles, SAMPLE_TOTAL, points_within_tile)
    flat_index = obs_index.reshape(number_tiles, OBS)

    def equivalents(region_pair):
        states, cell_index = region_pair
        picked = jnp.take(states, cell_index, axis=1)
        centre = lax.optimization_barrier(jnp.mean(picked, axis=0))
        return ((picked - centre).astype(jnp.bfloat16), centre)
    anomaly_obs, obs_mean = lax.map(equivalents, (vertical_strips, flat_index))
    innovation = lax.optimization_barrier((obs_value.reshape(number_tiles, OBS) - obs_mean).astype(jnp.bfloat16))
    weights = obs_weight.reshape(number_tiles, OBS).astype(jnp.float32)
    row_pos = (flat_index // TILE_WIDTH).astype(jnp.float32)

    def padded_blocks(array):
        shaped = array.reshape((N_SPACE, lateral_tiles) + array.shape[1:])
        return jnp.pad(shaped, ((1, 1),) + ((0, 0),) * (shaped.ndim - 1))
    near_obs = padded_blocks(anomaly_obs)
    near_weight = padded_blocks(weights)
    near_innov = padded_blocks(innovation)
    near_rows = padded_blocks(row_pos)
    row_span = float(STRIP_HEIGHT)
    identity_k = jnp.eye(SAMPLE_TOTAL, dtype=jnp.float32)

    def analyse(region):
        block_row = region // lateral_tiles
        block_col = region % lateral_tiles
        zero_index = block_row * 0

        def pick(array):
            starts = (block_row, block_col) + (zero_index,) * (array.ndim - 2)
            extent = (3, 1) + array.shape[2:]
            return lax.dynamic_slice(array, starts, extent)[:, 0]
        obs_three = pick(near_obs)
        weight_three = pick(near_weight)
        innov_three = pick(near_innov).astype(jnp.float32)
        rows_three = pick(near_rows)
        weight_sets = (weight_three[0] * taper_above(rows_three[0], row_span), weight_three[1], weight_three[2] * taper_below(rows_three[2], row_span))
        curvature = (SAMPLE_TOTAL - 1.0) * identity_k
        right_side = jnp.zeros((SAMPLE_TOTAL,), jnp.float32)
        for block_index in range(3):
            scaled = (obs_three[block_index].astype(jnp.float32) * weight_sets[block_index]).astype(jnp.bfloat16)
            curvature = curvature + lax.dot_general(scaled, obs_three[block_index], (((1,), (1,)), ((), ())), preferred_element_type=jnp.float32)
            right_side = right_side + jnp.dot(obs_three[block_index].astype(jnp.float32), weight_sets[block_index] * innov_three[block_index], precision=highest)
        frobenius = jnp.sqrt(jnp.sum(curvature * curvature))
        iterate = curvature / frobenius
        inverse = identity_k
        for sweep_index in range(ITERS):
            middle = 1.5 * identity_k - 0.5 * jnp.dot(inverse, iterate, precision=highest)
            iterate = jnp.dot(iterate, middle, precision=highest)
            inverse = jnp.dot(middle, inverse, precision=highest)
        spread = inverse * (jnp.sqrt(SAMPLE_TOTAL - 1.0) / jnp.sqrt(frobenius))
        mean_shift = jnp.dot(inverse, jnp.dot(inverse, right_side, precision=highest), precision=highest) / frobenius
        transform = spread + mean_shift[:, None]
        states = lax.dynamic_index_in_dim(vertical_strips, region, 0, keepdims=False)
        centre = lax.optimization_barrier(jnp.mean(states, axis=0, keepdims=True))
        anomalies = states - centre
        return centre + lax.dot_general(transform, anomalies, (((0,), (0,)), ((), ())), precision=highest)
    analysed = lax.map(analyse, jnp.arange(number_tiles, dtype=jnp.int32))
    return analysed.reshape(N_SPACE, lateral_tiles, SAMPLE_TOTAL, STRIP_HEIGHT, TILE_WIDTH).transpose(2, 0, 3, 1, 4).reshape(SAMPLE_TOTAL, ROWS, COLS)
```

```python
import functools
import math

import jax
import jax.numpy as jnp
from jax import lax
from jax.experimental import pallas as pl
from jax.experimental.pallas import tpu as pltpu
from jax.sharding import PartitionSpec as P

STEPS = 8
ITERS = 6
REGION_COLS = 128
MESH = pl.DeviceIdType.MESH
F32 = jnp.float32
BF16 = jnp.bfloat16
NN = (((1,), (0,)), ((), ()))
NT = (((1,), (1,)), ((), ()))


def dot(a, b, dims=NN):
    return lax.dot_general(a, b, dims, preferred_element_type=F32)


def split(value, pieces):
    out = []
    for _ in range(pieces):
        part = value.astype(BF16)
        out.append(part)
        value = value - part.astype(F32)
    return out


def product(a, b):
    (ah, al), (bh, bl) = a, b
    return dot(
        jnp.concatenate([ah, ah, al], axis=1), jnp.concatenate([bh, bl, bh], axis=0)
    )


def stacked(rows, height, width):
    place = lax.broadcasted_iota(jnp.int32, (height, width), 0)
    out = jnp.zeros((height, width), F32)
    for i, row in enumerate(rows):
        out = jnp.where(place == i, jnp.broadcast_to(row, (height, width)), out)
    return out


def cycle(
    x_ref, drive_ref, y_ref, idx_ref, w_ref,
    dev_out, mean_out,
    state, drive, halo, edge, sums_s, centre_s, send_dev, a_hi, scaled, own_mat, own_vec, near_out, near_in,
    y_hi, y_lo, z_hi, z_lo, ret_dev, ret_mean,
    load_sem, halo_send, halo_recv, fwd_send, fwd_recv, sums_send, sums_recv,
    near_send, near_recv, ret_send, ret_recv, retm_send, retm_recv, keep_sem,
):
    groups = lax.axis_size("member")
    blocks = lax.axis_size("space")
    me = lax.axis_index("member")
    here = lax.axis_index("space")
    _, height, members, cols = state.shape
    regions = idx_ref.shape[0]
    half = members // 2
    everyone = members * groups
    has_above = here > 0
    has_below = here < blocks - 1

    load = pltpu.make_async_copy(x_ref, state.at[0], load_sem)
    load.start()

    barrier = pltpu.get_barrier_semaphore()

    @pl.when(has_above)
    def _():
        pl.semaphore_signal(barrier, inc=1, device_id={"space": here - 1}, device_id_type=MESH)

    @pl.when(has_below)
    def _():
        pl.semaphore_signal(barrier, inc=1, device_id={"space": here + 1}, device_id_type=MESH)

    for k in range(1, groups):
        pl.semaphore_signal(
            barrier, inc=1, device_id={"member": lax.rem(me + k, groups)}, device_id_type=MESH
        )

    for r in range(height):
        drive[r] = jnp.broadcast_to(2.0 * drive_ref[r : r + 1, :], (16, cols))

    @pl.when(jnp.logical_not(has_above))
    def _():
        halo[:, 0] = jnp.zeros(halo[:, 0].shape, BF16)

    @pl.when(jnp.logical_not(has_below))
    def _():
        halo[:, 1] = jnp.zeros(halo[:, 1].shape, BF16)

    sides_here = has_above.astype(jnp.int32) + has_below.astype(jnp.int32)
    pl.semaphore_wait(barrier, groups - 1 + sides_here)
    load.wait()

    def halo_copy(s, d, h):
        target = here + 1 if d == 0 else here - 1
        return pltpu.make_async_remote_copy(
            src_ref=edge.at[s, d, h],
            dst_ref=halo.at[s, d, h],
            send_sem=halo_send.at[s, d, h],
            recv_sem=halo_recv.at[s, d, h],
            device_id={"space": target},
            device_id_type=MESH,
        )

    def send_edges(s, slot, h):
        for d, row, wanted in ((0, height - 1, has_below), (1, 0, has_above)):
            edge[s, d, h] = state[slot, row, h * half : (h + 1) * half, :].astype(BF16)

            @pl.when(wanted)
            def _():
                halo_copy(s, d, h).start()

    def updated(x, north, south, push):
        east = pltpu.roll(x, cols - 1, 1)
        west = pltpu.roll(x, 1, 1)
        return 0.05 * (
            x * (1.0 + ((west - east) + (north - south)))
            + ((east + west) + (8.0 * (north + south) + push))
        )

    def step(s, carry):
        now = lax.rem(s, 2)
        later = 1 - now
        for h in range(2):
            @pl.when(has_above)
            def _():
                halo_copy(s, 0, h).wait_recv()

            @pl.when(has_below)
            def _():
                halo_copy(s, 1, h).wait_recv()

            def edges(t, carry):
                at = pl.multiple_of(t * 16, 16)
                m = pl.ds(pl.multiple_of(h * half + t * 16, 16), 16)
                x = state[now, 0, m, :]
                north = halo[s, 0, h, pl.ds(at, 16), :].astype(F32)
                state[later, 0, m, :] = updated(x, north, state[now, 1, m, :], drive[0])
                x = state[now, height - 1, m, :]
                south = halo[s, 1, h, pl.ds(at, 16), :].astype(F32)
                state[later, height - 1, m, :] = updated(
                    x, state[now, height - 2, m, :], south, drive[height - 1]
                )
                return carry

            lax.fori_loop(0, half // 16, edges, 0)

            @pl.when(s + 1 < STEPS)
            def _():
                send_edges(s + 1, later, h)

            def inner(i, carry):
                r = 1 + i // (half // 16)
                t = i % (half // 16)
                m = pl.ds(pl.multiple_of(h * half + t * 16, 16), 16)
                state[later, r, m, :] = updated(
                    state[now, r, m, :], state[now, r - 1, m, :], state[now, r + 1, m, :], drive[r]
                )
                return carry

            lax.fori_loop(0, (height - 2) * (half // 16), inner, 0)
        return carry

    send_edges(0, 0, 0)
    send_edges(0, 0, 1)
    lax.fori_loop(0, STEPS, step, 0)
    last = STEPS % 2

    def sums_copy(q, p):
        return pltpu.make_async_remote_copy(
            src_ref=sums_s.at[me], dst_ref=sums_s.at[p],
            send_sem=sums_send.at[q], recv_sem=sums_recv.at[p],
            device_id={"member": q}, device_id_type=MESH)

    def add_members(r, carry):
        sums_s[me, pl.ds(r, 1), :] = jnp.sum(state[last, r], axis=0, keepdims=True)
        return carry

    lax.fori_loop(0, height, add_members, 0)
    for k in range(1, groups):
        sums_copy(lax.rem(me + k, groups), me).start()
    for k in range(1, groups):
        peer = lax.rem(me + k, groups)
        sums_copy(peer, peer).wait_recv()
    total = sums_s[0]
    for p in range(1, groups):
        total = total + sums_s[p]
    centre_s[...] = total * (1.0 / everyone)

    def fwd_copy(q, p, g):
        rows = pl.ds(pl.multiple_of(p * members, members), members)
        return pltpu.make_async_remote_copy(
            src_ref=send_dev.at[q, g], dst_ref=a_hi.at[g, rows, :],
            send_sem=fwd_send.at[q, g], recv_sem=fwd_recv.at[p, g],
            device_id={"member": q}, device_id_type=MESH)

    for g in range(regions):
        def pack(q, carry):
            start = pl.multiple_of((q * regions + g) * REGION_COLS, REGION_COLS)
            for r in range(height):
                x = state[last, r, :, pl.ds(start, REGION_COLS)]
                mean = centre_s[r : r + 1, pl.ds(start, REGION_COLS)]
                send_dev[q, g, :, r * REGION_COLS : (r + 1) * REGION_COLS] = (x - mean).astype(BF16)
            return carry

        lax.fori_loop(0, groups, pack, 0)
        for k in range(1, groups):
            fwd_copy(lax.rem(me + k, groups), me, g).start()
        a_hi[g, pl.ds(pl.multiple_of(me * members, members), members), :] = send_dev[me, g]

    row_iota = lax.broadcasted_iota(jnp.int32, (height, REGION_COLS), 0).astype(F32)
    span = float(height)
    from_above = span - row_iota
    from_below = row_iota + 1.0
    taper_down = jnp.exp(-2.0 * from_above * from_above / (span * span))
    taper_up = jnp.exp(-2.0 * from_below * from_below / (span * span))

    def near_copy(g, d):
        target = here + 1 if d == 0 else here - 1
        return pltpu.make_async_remote_copy(
            src_ref=near_out.at[g, d], dst_ref=near_in.at[g, d],
            send_sem=near_send.at[g, d], recv_sem=near_recv.at[g, d],
            device_id={"space": target}, device_id_type=MESH)

    def centre_of(g):
        start = pl.multiple_of((me * regions + g) * REGION_COLS, REGION_COLS)
        return centre_s[:, pl.ds(start, REGION_COLS)]

    def curve(g, carry):
        for k in range(1, groups):
            peer = lax.rem(me + k, groups)
            fwd_copy(peer, peer, g).wait_recv()
        centre = centre_of(g)
        cells = idx_ref[pl.ds(g, 1), :]
        count = cells.shape[1]
        in_row = (
            lax.broadcasted_iota(jnp.int32, (height, count), 0) == cells // REGION_COLS
        ).astype(F32)
        in_col = (
            lax.broadcasted_iota(jnp.int32, (REGION_COLS, count), 0) == cells % REGION_COLS
        ).astype(F32).astype(BF16)
        centre_parts = jnp.concatenate(
            [piece.astype(F32) for piece in split(centre, 3)], axis=0
        ).astype(BF16)
        at_cols = dot(centre_parts, in_col)
        at_cols = at_cols[:height] + at_cols[height : 2 * height] + at_cols[2 * height :]
        obs_mean = jnp.sum(at_cols * in_row, axis=0, keepdims=True)
        innovation = (y_ref[pl.ds(g, 1), :] - obs_mean).astype(BF16).astype(F32)
        weight = w_ref[pl.ds(g, 1), :]
        push_hi, push_lo = split(weight * innovation, 2)
        sums = dot(
            jnp.concatenate(
                [in_row * weight, in_row * push_hi.astype(F32), in_row * push_lo.astype(F32)], axis=0
            ).astype(BF16),
            in_col,
            NT,
        )
        weights = sums[:height]
        pushes = sums[height : 2 * height] + sums[2 * height :]
        weights_down, weights_up = weights * taper_down, weights * taper_up
        pieces = []
        for values in (pushes, pushes * taper_down, pushes * taper_up):
            pieces.extend(piece.astype(F32) for piece in split(values, 3))
        for r in range(height):
            at = slice(r * REGION_COLS, (r + 1) * REGION_COLS)
            a = a_hi[g, :, at].astype(F32)
            for i, values in enumerate((weights, weights_down, weights_up)):
                scaled[i * everyone : (i + 1) * everyone, at] = (a * values[r : r + 1, :]).astype(BF16)
            scaled[3 * everyone :, at] = stacked(
                [piece[r : r + 1, :] for piece in pieces], 16, REGION_COLS
            ).astype(BF16)
        sums_k = dot(scaled[...], a_hi[g], NT)
        vectors = sums_k[3 * everyone :]
        vec = [vectors[3 * i : 3 * i + 1] + vectors[3 * i + 1 : 3 * i + 2] + vectors[3 * i + 2 : 3 * i + 3] for i in range(3)]
        own_mat[g] = sums_k[:everyone]
        own_vec[g] = jnp.broadcast_to(vec[0], (8, everyone))
        for d, wanted in ((0, has_below), (1, has_above)):
            near_out[g, d, :everyone, :] = sums_k[(d + 1) * everyone : (d + 2) * everyone].astype(BF16)
            near_out[g, d, everyone:, :] = stacked(
                [piece.astype(F32) for piece in split(vec[d + 1], 2)], 16, everyone
            ).astype(BF16)

            @pl.when(wanted)
            def _():
                near_copy(g, d).start()
        return carry

    lax.fori_loop(0, regions, curve, 0)

    @pl.when(jnp.logical_not(has_above))
    def _():
        near_in[:, 0] = jnp.zeros(near_in[:, 0].shape, BF16)

    @pl.when(jnp.logical_not(has_below))
    def _():
        near_in[:, 1] = jnp.zeros(near_in[:, 1].shape, BF16)

    def ret_copies(q, g):
        common = dict(device_id={"member": q}, device_id_type=MESH)
        return (
            pltpu.make_async_remote_copy(
                src_ref=ret_dev.at[q, g], dst_ref=dev_out.at[me, g],
                send_sem=ret_send.at[q, g], recv_sem=ret_recv.at[me, g], **common),
            pltpu.make_async_remote_copy(
                src_ref=ret_mean.at[g], dst_ref=mean_out.at[me, g],
                send_sem=retm_send.at[q, g], recv_sem=retm_recv.at[me, g], **common),
        )

    def ret_arrivals(p, g):
        common = dict(device_id={"member": p}, device_id_type=MESH)
        return (
            pltpu.make_async_remote_copy(
                src_ref=ret_dev.at[p, g], dst_ref=dev_out.at[p, g],
                send_sem=ret_send.at[p, g], recv_sem=ret_recv.at[p, g], **common),
            pltpu.make_async_remote_copy(
                src_ref=ret_mean.at[g], dst_ref=mean_out.at[p, g],
                send_sem=retm_send.at[p, g], recv_sem=retm_recv.at[p, g], **common),
        )

    def kept(g):
        return (
            pltpu.make_async_copy(ret_dev.at[me, g], dev_out.at[me, g], keep_sem.at[g, 0]),
            pltpu.make_async_copy(ret_mean.at[g], mean_out.at[me, g], keep_sem.at[g, 1]),
        )

    square = (everyone, everyone)
    eye = (
        lax.broadcasted_iota(jnp.int32, square, 0) == lax.broadcasted_iota(jnp.int32, square, 1)
    )
    pair = 2 if regions % 2 == 0 else 1

    def solve(j, carry):
        def put(hi, lo, l, value):
            hi[l], lo[l] = split(value, 2)

        def middle_of(product_zy):
            return jnp.where(eye, 1.5, 0.0) - 0.5 * product_zy

        sides, norms = [], []
        for l in range(pair):
            g = j * pair + l

            @pl.when(has_above)
            def _():
                near_copy(g, 0).wait_recv()

            @pl.when(has_below)
            def _():
                near_copy(g, 1).wait_recv()

        for l in range(pair):
            g = j * pair + l
            matrix = own_mat[g] + jnp.where(eye, everyone - 1.0, 0.0)
            side = own_vec[g, 0:1, :]
            for d in range(2):
                matrix = matrix + near_in[g, d, :everyone, :].astype(F32)
                tail = near_in[g, d, everyone:, :].astype(F32)
                side = side + tail[0:1] + tail[1:2]
            norm = jnp.sqrt(jnp.sum(matrix * matrix, keepdims=True))
            sides.append(side)
            norms.append(norm)
            iterate = matrix / norm
            middle = middle_of(iterate)
            z = split(middle, 2)
            z_hi[l], z_lo[l] = z
            put(y_hi, y_lo, l, product(split(iterate, 2), z))

        def sweep(i, carry):
            middles = [
                split(middle_of(product((z_hi[l], z_lo[l]), (y_hi[l], y_lo[l]))), 2)
                for l in range(pair)
            ]
            ys = [product((y_hi[l], y_lo[l]), middles[l]) for l in range(pair)]
            zs = [product(middles[l], (z_hi[l], z_lo[l])) for l in range(pair)]
            for l in range(pair):
                put(y_hi, y_lo, l, ys[l])
                put(z_hi, z_lo, l, zs[l])
            return carry

        lax.fori_loop(0, ITERS - 2, sweep, 0)
        middles = [
            split(middle_of(product((z_hi[l], z_lo[l]), (y_hi[l], y_lo[l]))), 2)
            for l in range(pair)
        ]
        inverses = [product(middles[l], (z_hi[l], z_lo[l])) for l in range(pair)]
        for l in range(pair):
            g = j * pair + l
            zt = split(inverses[l].T, 2)

            def apply(row):
                parts = stacked([p.astype(F32) for p in split(row, 3)], 16, everyone).astype(BF16)
                out = dot(parts, zt[0]) + dot(parts, zt[1])
                return out[0:1] + out[1:2] + out[2:3]

            shift = apply(apply(sides[l])) / norms[l]
            parts = stacked([p.astype(F32) for p in split(shift, 3)], 16, everyone).astype(BF16)
            moved = dot(parts, a_hi[g])
            moved = moved[0:1] + moved[1:2] + moved[2:3]
            gain = math.sqrt(everyone - 1.0) / jnp.sqrt(norms[l])
            deviation = gain * (dot(zt[0], a_hi[g]) + dot(zt[1], a_hi[g]))
            centre = centre_of(g)
            for r in range(height):
                at = slice(r * REGION_COLS, (r + 1) * REGION_COLS)
                ret_mean[g, r : r + 1, :] = centre[r : r + 1, :] + moved[:, at]
                for q in range(groups):
                    ret_dev[q, g, r] = deviation[q * members : (q + 1) * members, at].astype(BF16)
            for k in range(1, groups):
                for copy in ret_copies(lax.rem(me + k, groups), g):
                    copy.start()
            for copy in kept(g):
                copy.start()
        return carry

    lax.fori_loop(0, regions // pair, solve, 0)

    def finish(g, carry):
        for copy in kept(g):
            copy.wait()
        for k in range(1, groups):
            peer = lax.rem(me + k, groups)
            for copy in ret_arrivals(peer, g):
                copy.wait_recv()
            for copy in ret_copies(peer, g) + (fwd_copy(peer, me, g),):
                copy.wait_send()
        for d, wanted in ((0, has_below), (1, has_above)):
            @pl.when(wanted)
            def _():
                near_copy(g, d).wait_send()
        return carry

    lax.fori_loop(0, regions, finish, 0)
    for k in range(1, groups):
        sums_copy(lax.rem(me + k, groups), me).wait_send()

    def drain(s, carry):
        for h in range(2):
            for d, wanted in ((0, has_below), (1, has_above)):
                @pl.when(wanted)
                def _():
                    halo_copy(s, d, h).wait_send()
        return carry

    lax.fori_loop(0, STEPS, drain, 0)


def local(prior_samples, external_drive, obs_value, obs_index, obs_weight):
    members, height, cols = prior_samples.shape
    groups = lax.axis_size("member")
    regions, count = obs_index.shape[1:]
    everyone = members * groups
    cells = height * REGION_COLS
    half = members // 2
    vmem = pl.BlockSpec(memory_space=pltpu.VMEM)
    anywhere = pl.BlockSpec(memory_space=pl.ANY)
    dma = pltpu.SemaphoreType.DMA
    dev_shape = (groups, regions, height, members, REGION_COLS)
    mean_shape = (groups, regions, height, REGION_COLS)
    matrices = (2, everyone, everyone)
    dev, mean = pl.pallas_call(
        cycle,
        out_shape=(
            jax.ShapeDtypeStruct(dev_shape, BF16),
            jax.ShapeDtypeStruct(mean_shape, F32),
        ),
        in_specs=[anywhere, vmem, vmem, vmem, vmem],
        out_specs=(anywhere, anywhere),
        scratch_shapes=[
            pltpu.VMEM((2, height, members, cols), F32),
            pltpu.VMEM((height, 16, cols), F32),
            pltpu.VMEM((STEPS, 2, 2, half, cols), BF16),
            pltpu.VMEM((STEPS, 2, 2, half, cols), BF16),
            pltpu.VMEM((groups, height, cols), F32),
            pltpu.VMEM((height, cols), F32),
            pltpu.VMEM((groups, regions, members, cells), BF16),
            pltpu.VMEM((regions, everyone, cells), BF16),
            pltpu.VMEM((3 * everyone + 16, cells), BF16),
            pltpu.VMEM((regions, everyone, everyone), F32),
            pltpu.VMEM((regions, 8, everyone), F32),
            pltpu.VMEM((regions, 2, everyone + 16, everyone), BF16),
            pltpu.VMEM((regions, 2, everyone + 16, everyone), BF16),
            pltpu.VMEM(matrices, BF16),
            pltpu.VMEM(matrices, BF16),
            pltpu.VMEM(matrices, BF16),
            pltpu.VMEM(matrices, BF16),
            pltpu.VMEM(dev_shape, BF16),
            pltpu.VMEM(mean_shape[1:], F32),
            dma,
            dma((STEPS, 2, 2)),
            dma((STEPS, 2, 2)),
            dma((groups, regions)),
            dma((groups, regions)),
            dma((groups,)),
            dma((groups,)),
            dma((regions, 2)),
            dma((regions, 2)),
            dma((groups, regions)),
            dma((groups, regions)),
            dma((groups, regions)),
            dma((groups, regions)),
            dma((regions, 2)),
        ],
        compiler_params=pltpu.CompilerParams(
            collective_id=0, has_side_effects=True, vmem_limit_bytes=56 * 1024 * 1024
        ),
        cost_estimate=pl.CostEstimate(
            flops=20_000_000_000, bytes_accessed=20_000_000, transcendentals=0
        ),
    )(
        prior_samples.transpose(1, 0, 2),
        external_drive,
        obs_value[0],
        obs_index[0],
        obs_weight[0].astype(F32),
    )
    out = dev.astype(F32) + mean[:, :, :, None, :]
    return out.transpose(3, 2, 0, 1, 4).reshape(members, height, cols)


def solution(mesh):
    return jax.shard_map(
        local,
        mesh=mesh,
        in_specs=(
            P("member", "space", None),
            P("space", None),
            P("space", "member", None),
            P("space", "member", None),
            P("space", "member", None),
        ),
        out_specs=P("member", "space", None),
        check_vma=False,
    )
```

```python
import functools
import math

import jax
import jax.numpy as jnp
from jax import lax
from jax.experimental import pallas as pl
from jax.experimental.pallas import tpu as pltpu
from jax.sharding import PartitionSpec as P

STEPS = 8
ITERS = 6
REGION_COLS = 128
MESH = pl.DeviceIdType.MESH
F32 = jnp.float32
BF16 = jnp.bfloat16
NN = (((1,), (0,)), ((), ()))
NT = (((1,), (1,)), ((), ()))


def dot(a, b, dims=NN):
    return lax.dot_general(a, b, dims, preferred_element_type=F32)


def split(value, pieces):
    out = []
    for _ in range(pieces):
        part = value.astype(BF16)
        out.append(part)
        value = value - part.astype(F32)
    return out


def product(a, b):
    (ah, al), (bh, bl) = a, b
    return dot(
        jnp.concatenate([ah, ah, al], axis=1), jnp.concatenate([bh, bl, bh], axis=0)
    )


def stacked(rows, height, width):
    place = lax.broadcasted_iota(jnp.int32, (height, width), 0)
    out = jnp.zeros((height, width), F32)
    for i, row in enumerate(rows):
        out = jnp.where(place == i, jnp.broadcast_to(row, (height, width)), out)
    return out


def cycle(
    x_ref, drive_ref, y_ref, idx_ref, w_ref,
    dev_out, mean_out,
    x_buf, w_s, state, drive, halo, edge, sums_s, centre_s, send_dev, a_hi, scaled, own_mat, own_vec, near_out, near_in,
    y_hi, y_lo, z_hi, z_lo, ret_dev, ret_mean,
    load_sem, halo_send, halo_recv, fwd_send, fwd_recv, sums_send, sums_recv,
    near_send, near_recv, ret_send, ret_recv, retm_send, retm_recv, keep_sem,
):
    groups = lax.axis_size("member")
    blocks = lax.axis_size("space")
    me = lax.axis_index("member")
    here = lax.axis_index("space")
    _, height, members, cols = state.shape
    regions = idx_ref.shape[0]
    half = members // 2
    everyone = members * groups
    has_above = here > 0
    has_below = here < blocks - 1

    cut = half * height
    tiles = cols // REGION_COLS

    def load(h, c):
        rows = slice(h * cut, (h + 1) * cut)
        at = pl.ds(pl.multiple_of(c * REGION_COLS, REGION_COLS), REGION_COLS)
        return pltpu.make_async_copy(x_ref.at[rows, at], x_buf.at[c, rows], load_sem.at[h, c])

    for h in range(2):
        def begin(c, carry):
            load(h, c).start()
            return carry

        lax.fori_loop(0, tiles, begin, 0)

    barrier = pltpu.get_barrier_semaphore()

    @pl.when(has_above)
    def _():
        pl.semaphore_signal(barrier, inc=1, device_id={"space": here - 1}, device_id_type=MESH)

    @pl.when(has_below)
    def _():
        pl.semaphore_signal(barrier, inc=1, device_id={"space": here + 1}, device_id_type=MESH)

    for k in range(1, groups):
        pl.semaphore_signal(
            barrier, inc=1, device_id={"member": lax.rem(me + k, groups)}, device_id_type=MESH
        )

    for r in range(height):
        drive[r] = jnp.broadcast_to(2.0 * drive_ref[r : r + 1, :], (16, cols))

    @pl.when(jnp.logical_not(has_above))
    def _():
        halo[:, 0] = jnp.zeros(halo[:, 0].shape, BF16)

    @pl.when(jnp.logical_not(has_below))
    def _():
        halo[:, 1] = jnp.zeros(halo[:, 1].shape, BF16)

    w_s[...] = w_ref[0].astype(F32)
    sides_here = has_above.astype(jnp.int32) + has_below.astype(jnp.int32)
    pl.semaphore_wait(barrier, groups - 1 + sides_here)

    def halo_copy(s, d, h):
        target = here + 1 if d == 0 else here - 1
        return pltpu.make_async_remote_copy(
            src_ref=edge.at[s, d, h],
            dst_ref=halo.at[s, d, h],
            send_sem=halo_send.at[s, d, h],
            recv_sem=halo_recv.at[s, d, h],
            device_id={"space": target},
            device_id_type=MESH,
        )

    def send_edges(s, slot, h):
        for d, row, wanted in ((0, height - 1, has_below), (1, 0, has_above)):
            edge[s, d, h] = state[slot, row, h * half : (h + 1) * half, :].astype(BF16)

            @pl.when(wanted)
            def _():
                halo_copy(s, d, h).start()

    def updated(x, north, south, push):
        east = pltpu.roll(x, cols - 1, 1)
        west = pltpu.roll(x, 1, 1)
        return 0.05 * (
            x * (1.0 + ((west - east) + (north - south)))
            + ((east + west) + (8.0 * (north + south) + push))
        )

    def step(s, carry):
        now = lax.rem(s, 2)
        later = 1 - now
        for h in range(2):
            @pl.when(has_above)
            def _():
                halo_copy(s, 0, h).wait_recv()

            @pl.when(has_below)
            def _():
                halo_copy(s, 1, h).wait_recv()

            def edges(t, carry):
                at = pl.multiple_of(t * 16, 16)
                m = pl.ds(pl.multiple_of(h * half + t * 16, 16), 16)
                x = state[now, 0, m, :]
                north = halo[s, 0, h, pl.ds(at, 16), :].astype(F32)
                state[later, 0, m, :] = updated(x, north, state[now, 1, m, :], drive[0])
                x = state[now, height - 1, m, :]
                south = halo[s, 1, h, pl.ds(at, 16), :].astype(F32)
                state[later, height - 1, m, :] = updated(
                    x, state[now, height - 2, m, :], south, drive[height - 1]
                )
                return carry

            lax.fori_loop(0, half // 16, edges, 0)

            @pl.when(s + 1 < STEPS)
            def _():
                send_edges(s + 1, later, h)

            def inner(i, carry):
                r = 1 + i // (half // 16)
                t = i % (half // 16)
                m = pl.ds(pl.multiple_of(h * half + t * 16, 16), 16)
                state[later, r, m, :] = updated(
                    state[now, r, m, :], state[now, r - 1, m, :], state[now, r + 1, m, :], drive[r]
                )
                return carry

            lax.fori_loop(0, (height - 2) * (half // 16), inner, 0)
        return carry

    def unfold(h, rows, wait):
        def tile(c, carry):
            if wait:
                load(h, c).wait()
            at = pl.ds(pl.multiple_of(c * REGION_COLS, REGION_COLS), REGION_COLS)
            for r in rows:
                state[0, r, h * half : (h + 1) * half, at] = x_buf[
                    c, pl.ds(h * cut + r, half, stride=height), :
                ]
            return carry

        lax.fori_loop(0, tiles, tile, 0)

    for h in range(2):
        unfold(h, (0, height - 1), True)
        send_edges(0, 0, h)
    for h in range(2):
        unfold(h, range(1, height - 1), False)
    lax.fori_loop(0, STEPS, step, 0)
    last = STEPS % 2

    def sums_copy(q, p):
        return pltpu.make_async_remote_copy(
            src_ref=sums_s.at[me], dst_ref=sums_s.at[p],
            send_sem=sums_send.at[q], recv_sem=sums_recv.at[p],
            device_id={"member": q}, device_id_type=MESH)

    def add_members(r, carry):
        sums_s[me, pl.ds(r, 1), :] = jnp.sum(state[last, r], axis=0, keepdims=True)
        return carry

    lax.fori_loop(0, height, add_members, 0)
    for k in range(1, groups):
        sums_copy(lax.rem(me + k, groups), me).start()
    for k in range(1, groups):
        peer = lax.rem(me + k, groups)
        sums_copy(peer, peer).wait_recv()
    total = sums_s[0]
    for p in range(1, groups):
        total = total + sums_s[p]
    centre_s[...] = total * (1.0 / everyone)

    def fwd_copy(q, p, g):
        rows = pl.ds(pl.multiple_of(p * members, members), members)
        return pltpu.make_async_remote_copy(
            src_ref=send_dev.at[q, g], dst_ref=a_hi.at[g, rows, :],
            send_sem=fwd_send.at[q, g], recv_sem=fwd_recv.at[p, g],
            device_id={"member": q}, device_id_type=MESH)

    for g in range(regions):
        def pack(q, carry):
            start = pl.multiple_of((q * regions + g) * REGION_COLS, REGION_COLS)
            for r in range(height):
                x = state[last, r, :, pl.ds(start, REGION_COLS)]
                mean = centre_s[r : r + 1, pl.ds(start, REGION_COLS)]
                send_dev[q, g, :, r * REGION_COLS : (r + 1) * REGION_COLS] = (x - mean).astype(BF16)
            return carry

        lax.fori_loop(0, groups, pack, 0)
        for k in range(1, groups):
            fwd_copy(lax.rem(me + k, groups), me, g).start()
        a_hi[g, pl.ds(pl.multiple_of(me * members, members), members), :] = send_dev[me, g]

    row_iota = lax.broadcasted_iota(jnp.int32, (height, REGION_COLS), 0).astype(F32)
    span = float(height)
    from_above = span - row_iota
    from_below = row_iota + 1.0
    taper_down = jnp.exp(-2.0 * from_above * from_above / (span * span))
    taper_up = jnp.exp(-2.0 * from_below * from_below / (span * span))

    def near_copy(g, d):
        target = here + 1 if d == 0 else here - 1
        return pltpu.make_async_remote_copy(
            src_ref=near_out.at[g, d], dst_ref=near_in.at[g, d],
            send_sem=near_send.at[g, d], recv_sem=near_recv.at[g, d],
            device_id={"space": target}, device_id_type=MESH)

    def centre_of(g):
        start = pl.multiple_of((me * regions + g) * REGION_COLS, REGION_COLS)
        return centre_s[:, pl.ds(start, REGION_COLS)]

    def curve(g, carry):
        centre = centre_of(g)
        cells = idx_ref[pl.ds(g, 1), :]
        count = cells.shape[1]
        in_row = (
            lax.broadcasted_iota(jnp.int32, (height, count), 0) == cells // REGION_COLS
        ).astype(F32)
        in_col = (
            lax.broadcasted_iota(jnp.int32, (REGION_COLS, count), 0) == cells % REGION_COLS
        ).astype(F32).astype(BF16)
        centre_parts = jnp.concatenate(
            [piece.astype(F32) for piece in split(centre, 3)], axis=0
        ).astype(BF16)
        at_cols = dot(centre_parts, in_col)
        at_cols = at_cols[:height] + at_cols[height : 2 * height] + at_cols[2 * height :]
        obs_mean = jnp.sum(at_cols * in_row, axis=0, keepdims=True)
        innovation = (y_ref[pl.ds(g, 1), :] - obs_mean).astype(BF16).astype(F32)
        weight = w_s[pl.ds(g, 1), :]
        push_hi, push_lo = split(weight * innovation, 2)
        sums = dot(
            jnp.concatenate(
                [in_row * weight, in_row * push_hi.astype(F32), in_row * push_lo.astype(F32)], axis=0
            ).astype(BF16),
            in_col,
            NT,
        )
        weights = sums[:height]
        pushes = sums[height : 2 * height] + sums[2 * height :]
        weights_down, weights_up = weights * taper_down, weights * taper_up
        pieces = []
        for values in (pushes, pushes * taper_down, pushes * taper_up):
            pieces.extend(piece.astype(F32) for piece in split(values, 3))
        for k in range(1, groups):
            peer = lax.rem(me + k, groups)
            fwd_copy(peer, peer, g).wait_recv()
        for r in range(height):
            at = slice(r * REGION_COLS, (r + 1) * REGION_COLS)
            a = a_hi[g, :, at].astype(F32)
            for i, values in enumerate((weights, weights_down, weights_up)):
                scaled[i * everyone : (i + 1) * everyone, at] = (a * values[r : r + 1, :]).astype(BF16)
            scaled[3 * everyone :, at] = stacked(
                [piece[r : r + 1, :] for piece in pieces], 16, REGION_COLS
            ).astype(BF16)
        sums_k = dot(scaled[...], a_hi[g], NT)
        vectors = sums_k[3 * everyone :]
        vec = [vectors[3 * i : 3 * i + 1] + vectors[3 * i + 1 : 3 * i + 2] + vectors[3 * i + 2 : 3 * i + 3] for i in range(3)]
        own_mat[g] = sums_k[:everyone]
        own_vec[g] = jnp.broadcast_to(vec[0], (8, everyone))
        for d, wanted in ((0, has_below), (1, has_above)):
            near_out[g, d, :everyone, :] = sums_k[(d + 1) * everyone : (d + 2) * everyone].astype(BF16)
            near_out[g, d, everyone:, :] = stacked(
                [piece.astype(F32) for piece in split(vec[d + 1], 2)], 16, everyone
            ).astype(BF16)

            @pl.when(wanted)
            def _():
                near_copy(g, d).start()
        return carry

    @pl.when(jnp.logical_not(has_above))
    def _():
        near_in[:, 0] = jnp.zeros(near_in[:, 0].shape, BF16)

    @pl.when(jnp.logical_not(has_below))
    def _():
        near_in[:, 1] = jnp.zeros(near_in[:, 1].shape, BF16)

    def ret_copies(q, g):
        common = dict(device_id={"member": q}, device_id_type=MESH)
        return (
            pltpu.make_async_remote_copy(
                src_ref=ret_dev.at[q, g], dst_ref=dev_out.at[me, g],
                send_sem=ret_send.at[q, g], recv_sem=ret_recv.at[me, g], **common),
            pltpu.make_async_remote_copy(
                src_ref=ret_mean.at[g], dst_ref=mean_out.at[me, g],
                send_sem=retm_send.at[q, g], recv_sem=retm_recv.at[me, g], **common),
        )

    def ret_arrivals(p, g):
        common = dict(device_id={"member": p}, device_id_type=MESH)
        return (
            pltpu.make_async_remote_copy(
                src_ref=ret_dev.at[p, g], dst_ref=dev_out.at[p, g],
                send_sem=ret_send.at[p, g], recv_sem=ret_recv.at[p, g], **common),
            pltpu.make_async_remote_copy(
                src_ref=ret_mean.at[g], dst_ref=mean_out.at[p, g],
                send_sem=retm_send.at[p, g], recv_sem=retm_recv.at[p, g], **common),
        )

    def kept(g):
        return (
            pltpu.make_async_copy(ret_dev.at[me, g], dev_out.at[me, g], keep_sem.at[g, 0]),
            pltpu.make_async_copy(ret_mean.at[g], mean_out.at[me, g], keep_sem.at[g, 1]),
        )

    square = (everyone, everyone)
    eye = (
        lax.broadcasted_iota(jnp.int32, square, 0) == lax.broadcasted_iota(jnp.int32, square, 1)
    )
    pair = 1

    def solve(j, carry):
        def put(hi, lo, l, value):
            hi[l], lo[l] = split(value, 2)

        def middle_of(product_zy):
            return jnp.where(eye, 1.5, 0.0) - 0.5 * product_zy

        sides, norms = [], []
        for l in range(pair):
            g = j * pair + l

            @pl.when(has_above)
            def _():
                near_copy(g, 0).wait_recv()

            @pl.when(has_below)
            def _():
                near_copy(g, 1).wait_recv()

        for l in range(pair):
            g = j * pair + l
            matrix = own_mat[g] + jnp.where(eye, everyone - 1.0, 0.0)
            side = own_vec[g, 0:1, :]
            for d in range(2):
                matrix = matrix + near_in[g, d, :everyone, :].astype(F32)
                tail = near_in[g, d, everyone:, :].astype(F32)
                side = side + tail[0:1] + tail[1:2]
            norm = jnp.sqrt(jnp.sum(matrix * matrix, keepdims=True))
            sides.append(side)
            norms.append(norm)
            iterate = matrix * (1.0 / norm)
            middle = middle_of(iterate)
            z = split(middle, 2)
            z_hi[l], z_lo[l] = z
            put(y_hi, y_lo, l, product(split(iterate, 2), z))

        def sweep(i, carry):
            middles = [
                split(middle_of(product((z_hi[l], z_lo[l]), (y_hi[l], y_lo[l]))), 2)
                for l in range(pair)
            ]
            ys = [product((y_hi[l], y_lo[l]), middles[l]) for l in range(pair)]
            zs = [product(middles[l], (z_hi[l], z_lo[l])) for l in range(pair)]
            for l in range(pair):
                put(y_hi, y_lo, l, ys[l])
                put(z_hi, z_lo, l, zs[l])
            return carry

        lax.fori_loop(0, ITERS - 2, sweep, 0)
        middles = [
            split(middle_of(product((z_hi[l], z_lo[l]), (y_hi[l], y_lo[l]))), 2)
            for l in range(pair)
        ]
        inverses = [product(middles[l], (z_hi[l], z_lo[l])) for l in range(pair)]
        for l in range(pair):
            g = j * pair + l
            zt = split(inverses[l].T, 2)

            def apply(row):
                parts = stacked([p.astype(F32) for p in split(row, 3)], 16, everyone).astype(BF16)
                out = dot(parts, zt[0]) + dot(parts, zt[1])
                return out[0:1] + out[1:2] + out[2:3]

            shift = apply(apply(sides[l])) / norms[l]
            parts = stacked([p.astype(F32) for p in split(shift, 3)], 16, everyone).astype(BF16)
            moved = dot(parts, a_hi[g])
            moved = moved[0:1] + moved[1:2] + moved[2:3]
            gain = math.sqrt(everyone - 1.0) / jnp.sqrt(norms[l])
            deviation = gain * (dot(zt[0], a_hi[g]) + dot(zt[1], a_hi[g]))
            centre = centre_of(g)
            for r in range(height):
                at = slice(r * REGION_COLS, (r + 1) * REGION_COLS)
                ret_mean[g, r : r + 1, :] = centre[r : r + 1, :] + moved[:, at]
                for q in range(groups):
                    ret_dev[q, g, r] = deviation[q * members : (q + 1) * members, at].astype(BF16)
            for k in range(1, groups):
                for copy in ret_copies(lax.rem(me + k, groups), g):
                    copy.start()
            for copy in kept(g):
                copy.start()
        return carry

    def advance(g, carry):
        @pl.when(g < regions)
        def _():
            curve(g, 0)

        @pl.when(g > 0)
        def _():
            solve(g - 1, 0)

        return carry

    lax.fori_loop(0, regions + 1, advance, 0)

    def finish(g, carry):
        for copy in kept(g):
            copy.wait()
        for k in range(1, groups):
            peer = lax.rem(me + k, groups)
            for copy in ret_arrivals(peer, g):
                copy.wait_recv()
            for copy in ret_copies(peer, g) + (fwd_copy(peer, me, g),):
                copy.wait_send()
        for d, wanted in ((0, has_below), (1, has_above)):
            @pl.when(wanted)
            def _():
                near_copy(g, d).wait_send()
        return carry

    lax.fori_loop(0, regions, finish, 0)
    for k in range(1, groups):
        sums_copy(lax.rem(me + k, groups), me).wait_send()

    def drain(s, carry):
        for h in range(2):
            for d, wanted in ((0, has_below), (1, has_above)):
                @pl.when(wanted)
                def _():
                    halo_copy(s, d, h).wait_send()
        return carry

    lax.fori_loop(0, STEPS, drain, 0)


def assemble(dev_ref, mean_ref, out_ref, folded, sem):
    _, regions, height, members, _ = dev_ref.shape
    p = pl.program_id(0)
    tiles = folded.shape[0]

    def store(c):
        at = pl.ds(pl.multiple_of(c * REGION_COLS, REGION_COLS), REGION_COLS)
        return pltpu.make_async_copy(folded.at[c], out_ref.at[:, at], sem.at[c])

    for g in range(regions):
        c = p * regions + g
        for r in range(height):
            folded[c, pl.ds(r, members, stride=height), :] = (
                dev_ref[0, g, r].astype(F32) + mean_ref[0, g, r : r + 1, :]
            )
        store(c).start()

    @pl.when(p == pl.num_programs(0) - 1)
    def _():
        for c in range(tiles):
            store(c).wait()


def local(prior_samples, external_drive, obs_value, obs_index, obs_weight):
    members, height, cols = prior_samples.shape
    groups = lax.axis_size("member")
    regions, count = obs_index.shape[1:]
    everyone = members * groups
    cells = height * REGION_COLS
    half = members // 2
    vmem = pl.BlockSpec(memory_space=pltpu.VMEM)
    anywhere = pl.BlockSpec(memory_space=pl.ANY)
    dma = pltpu.SemaphoreType.DMA
    dev_shape = (groups, regions, height, members, REGION_COLS)
    mean_shape = (groups, regions, height, REGION_COLS)
    matrices = (1, everyone, everyone)
    dev, mean = pl.pallas_call(
        cycle,
        out_shape=(
            jax.ShapeDtypeStruct(dev_shape, BF16),
            jax.ShapeDtypeStruct(mean_shape, F32),
        ),
        in_specs=[anywhere, vmem, vmem, vmem, vmem],
        out_specs=(anywhere, anywhere),
        scratch_shapes=[
            pltpu.VMEM((cols // REGION_COLS, members * height, REGION_COLS), F32),
            pltpu.VMEM((regions, count), F32),
            pltpu.VMEM((2, height, members, cols), F32),
            pltpu.VMEM((height, 16, cols), F32),
            pltpu.VMEM((STEPS, 2, 2, half, cols), BF16),
            pltpu.VMEM((STEPS, 2, 2, half, cols), BF16),
            pltpu.VMEM((groups, height, cols), F32),
            pltpu.VMEM((height, cols), F32),
            pltpu.VMEM((groups, regions, members, cells), BF16),
            pltpu.VMEM((regions, everyone, cells), BF16),
            pltpu.VMEM((3 * everyone + 16, cells), BF16),
            pltpu.VMEM((regions, everyone, everyone), F32),
            pltpu.VMEM((regions, 8, everyone), F32),
            pltpu.VMEM((regions, 2, everyone + 16, everyone), BF16),
            pltpu.VMEM((regions, 2, everyone + 16, everyone), BF16),
            pltpu.VMEM(matrices, BF16),
            pltpu.VMEM(matrices, BF16),
            pltpu.VMEM(matrices, BF16),
            pltpu.VMEM(matrices, BF16),
            pltpu.VMEM(dev_shape, BF16),
            pltpu.VMEM(mean_shape[1:], F32),
            dma((2, cols // REGION_COLS)),
            dma((STEPS, 2, 2)),
            dma((STEPS, 2, 2)),
            dma((groups, regions)),
            dma((groups, regions)),
            dma((groups,)),
            dma((groups,)),
            dma((regions, 2)),
            dma((regions, 2)),
            dma((groups, regions)),
            dma((groups, regions)),
            dma((groups, regions)),
            dma((groups, regions)),
            dma((regions, 2)),
        ],
        compiler_params=pltpu.CompilerParams(
            collective_id=0, has_side_effects=True, vmem_limit_bytes=56 * 1024 * 1024
        ),
        cost_estimate=pl.CostEstimate(
            flops=20_000_000_000, bytes_accessed=20_000_000, transcendentals=0
        ),
    )(
        prior_samples.reshape(members * height, cols),
        external_drive,
        obs_value[0],
        obs_index[0],
        obs_weight,
    )
    out = pl.pallas_call(
        assemble,
        grid=(groups,),
        out_shape=jax.ShapeDtypeStruct((members * height, cols), F32),
        in_specs=[
            pl.BlockSpec((1,) + dev_shape[1:], lambda p: (p, 0, 0, 0, 0)),
            pl.BlockSpec((1,) + mean_shape[1:], lambda p: (p, 0, 0, 0)),
        ],
        out_specs=anywhere,
        scratch_shapes=[
            pltpu.VMEM((cols // REGION_COLS, members * height, REGION_COLS), F32),
            dma((cols // REGION_COLS,)),
        ],
        compiler_params=pltpu.CompilerParams(vmem_limit_bytes=24 * 1024 * 1024),
        cost_estimate=pl.CostEstimate(flops=2_000_000, bytes_accessed=7_000_000, transcendentals=0),
    )(dev, mean)
    return out.reshape(members, height, cols)


def solution(mesh):
    return jax.shard_map(
        local,
        mesh=mesh,
        in_specs=(
            P("member", "space", None),
            P("space", None),
            P("space", "member", None),
            P("space", "member", None),
            P("space", "member", None),
        ),
        out_specs=P("member", "space", None),
        check_vma=False,
    )
```
